256 devices in a mesh: blk: 8 (over x, y_hi), dom: 32 (over z, y_lo, core).
Axes of the slice: x: 4, y: 4 (y_hi: 2, y_lo: 2; y = y_hi * 2 + y_lo), z: 8, core: 2. Of those that a mesh axis runs over, the one named last changes fastest.
Arguments:
- orbitals: float32 [8, 256, 256, 256], P('blk', 'dom'), may hold values from -7 to 7
- dielectric: float32 [256, 256, 256], P('dom'), may hold values from 1 to 10
Outputs:
- exchange: float32 [8, 256, 256, 256], P('blk', 'dom')
The draws below stay inside these ranges and needn't reach their ends.
All inputs are finite; a program needn't handle non-finite values.
Results may differ from the reference program's by a relative error of at most 0.0001.
Values sent between devices are 32-bit elements; how exact they have to be, the bound alone decides.
A program may use at most 128 MiB of HBM per device.

```python
import math
import jax
import jax.numpy as jnp
from jax import lax

NY = 256
NZ = 256
ITERS = 3
ORBS = 8
NX = 256


def draw_orbitals(key, part):
    fraction = jnp.arange(NX, dtype=jnp.float32) / max(NX - 1, 1)
    fraction = fraction.reshape(1, NX, 1, 1)
    pattern = jnp.clip(jax.random.normal(key, (ORBS, NX, NY, NZ), jnp.float32), -4.0, 4.0)
    envelope = jnp.power(3.0, fraction - 0.5)
    return (pattern * envelope).astype(jnp.float32)


def levels(rng, dims, cuts, least, high):
    level = 1.0
    for axis_at, shards_of in cuts:
        heights = jax.random.uniform(jax.random.fold_in(jax.random.fold_in(rng, 6), axis_at), (shards_of,), jnp.float32, least / len(cuts), high / len(cuts))
        level = level * jnp.repeat(jnp.exp(heights), dims[axis_at] // shards_of).reshape((-1,) + (1,) * (len(dims) - 1 - axis_at))
    return level


def setup_inputs(seed: int = 0) -> dict:
    arg_keys = jax.random.split(jax.random.key(seed), 3)
    orbitals = draw_orbitals(jax.random.fold_in(arg_keys[2], 71), 0)
    dielectric = jnp.clip(jnp.exp(math.log(10.0) - 2.3025851 * jax.random.uniform(arg_keys[1], (NX, NY, NZ), jnp.float32) ** levels(arg_keys[1], (NX, NY, NZ), ((0, 32),), -0.2, 0.2)), 1.0, 10.0)
    return {"orbitals": orbitals, "dielectric": dielectric}


FOUR_PI = 4.0 * math.pi


def face_weights(eps_pad):
    center = eps_pad[1:-1, 1:-1, 1:-1]
    return ((center + eps_pad[2:, 1:-1, 1:-1]) * 0.5,
            (center + eps_pad[:-2, 1:-1, 1:-1]) * 0.5,
            (center + eps_pad[1:-1, 2:, 1:-1]) * 0.5,
            (center + eps_pad[1:-1, :-2, 1:-1]) * 0.5,
            (center + eps_pad[1:-1, 1:-1, 2:]) * 0.5,
            (center + eps_pad[1:-1, 1:-1, :-2]) * 0.5)


def apply_operator(padded, weights):
    center = padded[:, 1:-1, 1:-1, 1:-1]
    result = weights[0] * (center - padded[:, 2:, 1:-1, 1:-1])
    result = result + weights[1] * (center - padded[:, :-2, 1:-1, 1:-1])
    result = result + weights[2] * (center - padded[:, 1:-1, 2:, 1:-1])
    result = result + weights[3] * (center - padded[:, 1:-1, :-2, 1:-1])
    result = result + weights[4] * (center - padded[:, 1:-1, 1:-1, 2:])
    result = result + weights[5] * (center - padded[:, 1:-1, 1:-1, :-2])
    return result


def inner_sum(first, second):
    return jnp.sum(first * second, axis=(1, 2, 3), keepdims=True)


def conjugate(right_side, weights):
    solution = jnp.zeros_like(right_side)
    residual = right_side
    direction = right_side
    norm_now = inner_sum(residual, residual)
    for iteration in range(ITERS):
        padded = jnp.pad(direction, ((0, 0), (1, 1), (1, 1), (1, 1)))
        applied = apply_operator(padded, weights)
        step_length = norm_now / inner_sum(direction, applied)
        solution = solution + step_length * direction
        residual = residual - step_length * applied
        norm_next = inner_sum(residual, residual)
        direction = residual + (norm_next / norm_now) * direction
        norm_now = norm_next
    return solution


def reference(orbitals, dielectric):
    weights = face_weights(jnp.pad(dielectric, 1))
    left_orbital = jnp.roll(orbitals, 1, axis=0)
    density = FOUR_PI * orbitals * left_orbital
    potential = lax.map(lambda single: conjugate(single[None], weights)[0], density)
    returned = jnp.roll(potential * orbitals, -1, axis=0)
    return -(potential * left_orbital + returned)
```

```python
import functools
import math

import jax
import jax.numpy as jnp
from jax import lax
from jax.experimental import pallas as pl
from jax.experimental.pallas import tpu as pltpu
from jax.sharding import PartitionSpec as P

FOUR_PI = 4.0 * math.pi
ITERS = 3
CHUNKS = 4
STRIP = 16
F32 = jnp.float32


def kernel(cx, cz, orb, eps, out, *scratch):
    (o, e, wx, wyp, wym, wzp, wzm, field, image, pack, rows, epack, erows, red, zin, yred, yin, far_out,
     near_out, u_out, u_in, near_s, near_r, third_s, eps_s, eps_r, plane_s, plane_r, row_s, row_r, z_s, z_r,
     y_s, y_r, out_s, out_r, u_s, u_r) = scratch
    planes, height, lanes = o.shape[1:]
    half = planes // 2
    step = half // CHUNKS
    blk, dom = lax.axis_index("blk"), lax.axis_index("dom")
    x, yh = blk // 2, blk % 2
    z, yl, core = dom // 4, (dom // 2) % 2, dom % 2
    y = 2 * yh + yl
    dx = 1 - 2 * yh

    def flip(value, by):
        return value + by - 2 * by * value if by else value

    def device(x_, yh_, z_, yl_, core_):
        x_, z_ = lax.rem(x_ + cx, cx), lax.rem(z_ + cz, cz)
        return {"blk": x_ * 2 + yh_, "dom": z_ * 4 + yl_ * 2 + core_}

    def remote(src, dst, send, recv, to):
        return pltpu.make_async_remote_copy(src_ref=src, dst_ref=dst, send_sem=send, recv_sem=recv, device_id=to)

    here = device(x, yh, z, yl, core)

    def arrived(dst, recv):
        pltpu.make_async_copy(dst, dst, recv).wait()

    def sent(src, send):
        pltpu.make_async_copy(src, src, send).wait()

    def either(is_self, src, dst, send, recv, to):
        @pl.when(is_self)
        def _():
            pltpu.make_async_copy(src, dst, recv).start()

        @pl.when(jnp.logical_not(is_self))
        def _():
            remote(src, dst, send, recv, to).start()

    barrier = pltpu.get_barrier_semaphore()
    partners = []
    for k in range(4):
        for cc in range(2):
            if k or cc:
                partners.append(device(x, flip(yh, k // 2), z, flip(yl, k % 2), flip(core, cc)))
    partners += [device(x + 1, yh, z, yl, core), device(x - 1, yh, z, yl, core)]
    partners += [device(x, yh, z + d, yl, core) for d in range(1, cz)]
    partners.append(device(x, yh, z + 2 * core - 1, yl, 1 - core))
    for k in range(2):
        for cc in range(2):
            partners.append(device(x + dx, 1 - yh, z, flip(yl, k), flip(core, cc)))
    for partner in partners:
        pl.semaphore_signal(barrier, inc=1, device_id=partner)
    pl.semaphore_wait(barrier, len(partners))

    own = core == yl
    y_other = lax.rem(y + 1 + 2 * core, 4)
    e_here = e.at[pl.ds(1 + half * core, half)]
    either(own, eps.at[:, pl.ds(height * y, height)], e_here, eps_s.at[0], eps_r.at[core],
           device(x, yh, z, yl, yl))
    remote(eps.at[:, pl.ds(height * y_other, height)], e_here, eps_s.at[1], eps_r.at[core],
           device(x, y_other // 2, z, lax.rem(y_other, 2), yl)).start()
    for chunk in range(CHUNKS):
        for k in (2, 3, 1, 0):
            jh, jl = flip(yh, k // 2), flip(yl, k % 2)
            src = orb.at[0, pl.ds(step * chunk, step), pl.ds(height * (2 * jh + jl), height)]
            dst = o.at[k // 2, pl.ds(half * core + step * chunk, step)]
            sems = near_s.at[k, chunk], near_r.at[k // 2, core, chunk]
            to = device(x, jh, z, jl, yl)
            if k:
                remote(src, dst, *sems, to).start()
            else:
                either(own, src, dst, *sems, to)

    def relay(t, carry):
        h, chunk = t // CHUNKS, lax.rem(t, CHUNKS)
        part = pl.ds(t * step, step)
        arrived(o.at[0, part], near_r.at[0, h, chunk])
        remote(o.at[0, part], o.at[2, part], third_s.at[h, chunk], near_r.at[2, h, chunk],
               device(x - dx, yh, z, yl, core)).start()
        return carry

    lax.fori_loop(0, 2 * CHUNKS, relay, 0)

    j_down, j_up = lax.rem(y + 1, 4), lax.rem(y + 3, 4)
    x_down = (x + jnp.where(y == 1, 1, 0), x + jnp.where(y == 1, 1, 0))
    x_up = x - jnp.where(y == 2, 1, 0)
    to_row = (
        (device(x, j_up // 2, z, lax.rem(j_up, 2), core), device(x, j_down // 2, z, lax.rem(j_down, 2), core)),
        (device(x_up, j_up // 2, z, lax.rem(j_up, 2), core),
         device(x_down[1], j_down // 2, z, lax.rem(j_down, 2), core)),
    )
    to_plane = (device(x, yh, z - 1 + core, yl, 1 - core), device(x, yh, z + core, yl, 1 - core))
    first_plane = jnp.logical_and(z == 0, core == 0)
    last_plane = jnp.logical_and(z == cz - 1, core == 1)

    def plane_copies(gen, lower, upper, lower_to, upper_to):
        return (remote(lower, upper_to, plane_s.at[gen, 0], plane_r.at[gen, 0], to_plane[0]),
                remote(upper, lower_to, plane_s.at[gen, 1], plane_r.at[gen, 1], to_plane[1]))

    def field_planes(gen):
        f = field.at[gen]
        return plane_copies(gen, f.at[:, 1], f.at[:, planes], f.at[:, 0], f.at[:, planes + 1])

    def field_rows(gen):
        return [remote(pack.at[gen, job, side], rows.at[gen, job, 1 - side], row_s.at[gen, job, side],
                       row_r.at[gen, job, 1 - side], to_row[job][side]) for job in range(2) for side in range(2)]

    def start(copies):
        for copy in copies:
            copy.start()

    def finish_rows(gen):
        for job in range(2):
            for side in range(2):
                arrived(rows.at[gen, job, side], row_r.at[gen, job, side])
        for side, edge in ((0, y == 0), (1, y == 3)):
            @pl.when(edge)
            def _():
                for job in range(2):
                    rows[gen, job, side] = jnp.zeros(rows.shape[3:], F32)

    def finish_planes(gen):
        f = field.at[gen]
        arrived(f.at[:, planes + 1], plane_r.at[gen, 0])
        arrived(f.at[:, 0], plane_r.at[gen, 1])
        for edge, at in ((first_plane, 0), (last_plane, planes + 1)):
            @pl.when(edge)
            def _():
                for job in range(2):
                    field[gen, job, at] = jnp.zeros((height, lanes), F32)

    def store_rows(gen, job, p, value):
        pack[gen, job, 0, p] = value[0:1]
        pack[gen, job, 1, p] = value[height - 1 : height]

    for h in range(2):
        arrived(e.at[pl.ds(1 + half * h, half)], eps_r.at[h])

    def pack_eps(p, carry):
        epack[0, p] = e[p + 1, 0:1]
        epack[1, p] = e[p + 1, height - 1 : height]
        return carry

    lax.fori_loop(0, planes, pack_eps, 0)
    eps_planes = plane_copies(ITERS, e.at[1], e.at[planes], e.at[0], e.at[planes + 1])
    eps_rows = [remote(epack.at[side], erows.at[1 - side], row_s.at[ITERS, 0, side], row_r.at[ITERS, 0, 1 - side],
                       to_row[0][side]) for side in range(2)]
    start(eps_planes)
    start(eps_rows)
    for side in range(2):
        arrived(erows.at[side], row_r.at[ITERS, 0, side])
    arrived(e.at[planes + 1], plane_r.at[ITERS, 0])
    arrived(e.at[0], plane_r.at[ITERS, 1])
    for edge, at in ((first_plane, 0), (last_plane, planes + 1)):
        @pl.when(edge)
        def _():
            e[at] = jnp.zeros((height, lanes), F32)
    for side, edge in ((0, y == 0), (1, y == 3)):
        @pl.when(edge)
        def _():
            erows[side] = jnp.zeros(erows.shape[1:], F32)

    row_at = lax.broadcasted_iota(jnp.int32, (STRIP, lanes), 0)
    lane_at = lax.broadcasted_iota(jnp.int32, (STRIP, lanes), 1)

    def four(value, before, after):
        below = jnp.where(row_at == STRIP - 1, after, pltpu.roll(value, STRIP - 1, 0))
        above = jnp.where(row_at == 0, before, pltpu.roll(value, 1, 0))
        right = jnp.where(lane_at == lanes - 1, 0.0, pltpu.roll(value, lanes - 1, 1))
        left = jnp.where(lane_at == 0, 0.0, pltpu.roll(value, 1, 1))
        return below, above, right, left

    def weigh(p, carry):
        for r in range(0, height, STRIP):
            s = pl.ds(r, STRIP)
            value = e[p + 1, s]
            before = e[p + 1, r - 1 : r] if r else erows[0, p]
            after = e[p + 1, r + STRIP : r + STRIP + 1] if r + STRIP < height else erows[1, p]
            below, above, right, left = four(value, before, after)
            wyp[p, s] = (value + below) * 0.5
            wym[p, s] = (value + above) * 0.5
            wzp[p, s] = (value + right) * 0.5
            wzm[p, s] = (value + left) * 0.5
            wx[p, s] = (value + e[p, s]) * 0.5
        return carry

    lax.fori_loop(0, planes, weigh, 0)
    wx[planes] = (e[planes] + e[planes + 1]) * 0.5

    def density(t, carry):
        h, chunk = t // CHUNKS, lax.rem(t, CHUNKS)
        part = pl.ds(t * step, step)
        arrived(o.at[1, part], near_r.at[1, h, chunk])
        arrived(o.at[2, part], near_r.at[2, h, chunk])
        for i in range(step):
            p = t * step + i
            far = FOUR_PI * o[1, p]
            for job, other in ((0, 0), (1, 2)):
                value = far * o[other, p]
                field[0, job, p + 1] = value
                store_rows(0, job, p, value)
        return carry

    lax.fori_loop(0, 2 * CHUNKS, density, 0)

    def folded(value):
        total = value[0:8]
        for r in range(8, STRIP, 8):
            total = total + value[r : r + 8]
        return total[:, : lanes // 2] + total[:, lanes // 2 :]

    def apply(gen, p, sums):
        sums = list(sums)
        for r in range(0, height, STRIP):
            s = pl.ds(r, STRIP)
            for job in range(2):
                value = field[gen, job, p + 1, s]
                before = field[gen, job, p + 1, r - 1 : r] if r else rows[gen, job, 0, p]
                after = field[gen, job, p + 1, r + STRIP : r + STRIP + 1] if r + STRIP < height else rows[gen, job, 1, p]
                below, above, right, left = four(value, before, after)
                result = wx[p + 1, s] * (value - field[gen, job, p + 2, s])
                result += wx[p, s] * (value - field[gen, job, p, s])
                result += wyp[p, s] * (value - below)
                result += wym[p, s] * (value - above)
                result += wzp[p, s] * (value - right)
                result += wzm[p, s] * (value - left)
                if gen < ITERS - 1:
                    image[gen, job, p, s] = result
                sums[2 * job] += folded(value * value)
                sums[2 * job + 1] += folded(value * result)
        return tuple(sums)

    half_lanes = lanes // 2
    tile_row = lax.broadcasted_iota(jnp.int32, (8, half_lanes), 0)

    def operator(gen):
        finish_rows(gen)
        sums = (jnp.zeros((8, half_lanes), F32),) * 4
        sums = lax.fori_loop(1, planes - 1, functools.partial(apply, gen), sums)
        finish_planes(gen)
        sums = lax.fori_loop(0, 2, lambda i, c: apply(gen, i * (planes - 1), c), sums)
        tile = jnp.zeros((8, half_lanes), F32)
        for q in range(4):
            tile = jnp.where(tile_row == q, jnp.sum(sums[q], axis=0, keepdims=True), tile)
        red[gen] = tile
        for d in range(1, cz):
            remote(red.at[gen], zin.at[gen, d - 1], z_s.at[gen, d - 1], z_r.at[gen, d - 1],
                   device(x, yh, z + d, yl, core)).start()
        for d in range(1, cz):
            arrived(zin.at[gen, d - 1], z_r.at[gen, d - 1])
            tile = tile + zin[gen, d - 1]
        yred[gen] = tile
        relations = [(x_, h, k, cc) for x_, h in ((0, 0), (0, 1), (1, 1)) for k in range(2) for cc in range(2)][1:]
        for at, (x_, h, k, cc) in enumerate(relations):
            remote(yred.at[gen], yin.at[gen, at], y_s.at[gen, at], y_r.at[gen, at],
                   device(x + dx * x_, flip(yh, h), z, flip(yl, k), flip(core, cc))).start()
        for at, (x_, h, k, cc) in enumerate(relations):
            arrived(yin.at[gen, at], y_r.at[gen, at])
            other = yin[gen, at]
            if h:
                other = jnp.where((tile_row // 2) == x_, other, 0.0)
            tile = tile + other
        total = jnp.broadcast_to(jnp.sum(tile, axis=1, keepdims=True), (8, half_lanes))
        return [(total[2 * job : 2 * job + 1], total[2 * job + 1 : 2 * job + 2]) for job in range(2)]

    def number(value):
        return value[0, 0]

    start(field_planes(0))
    start(field_rows(0))
    sums = operator(0)
    norm = [s[0] for s in sums]
    length = [s[0] / s[1] for s in sums]
    lengths, ratios = [length], []
    for gen in range(1, ITERS):
        by = [number(length[job]) for job in range(2)]
        beta = [number(ratios[-1][job]) for job in range(2)] if ratios else None

        def update(p, carry):
            for job in range(2):
                if beta is None:
                    moved = image[0, job, p]
                else:
                    moved = image[1, job, p] + beta[job] * image[0, job, p]
                value = field[gen - 1, job, p + 1] - by[job] * moved
                field[gen, job, p + 1] = value
                store_rows(gen, job, p, value)
            return carry

        lax.fori_loop(0, planes, update, 0)
        start(field_planes(gen))
        start(field_rows(gen))
        sums = operator(gen)
        ratio = [sums[job][0] / norm[job] for job in range(2)]
        length = [sums[job][0] / (sums[job][1] - ratio[job] * sums[job][0] / length[job]) for job in range(2)]
        norm = [s[0] for s in sums]
        lengths.append(length)
        ratios.append(ratio)

    coefficient = []
    for job in range(2):
        tail, of = None, [None] * ITERS
        for gen in reversed(range(ITERS)):
            tail = lengths[gen][job] if tail is None else lengths[gen][job] + tail * ratios[gen][job]
            of[gen] = number(tail)
        coefficient.append(of)

    def out_rows(h):
        return out.at[0, :, pl.ds(height * y, height)]

    def finish(t, carry):
        h, chunk = t // CHUNKS, lax.rem(t, CHUNKS)
        for i in range(step):
            p = t * step + i
            for r in range(0, height, 32):
                s = pl.ds(r, 32)
                potential = []
                for job in range(2):
                    value = coefficient[job][0] * field[0, job, p + 1, s]
                    for gen in range(1, ITERS):
                        value = value + coefficient[job][gen] * field[gen, job, p + 1, s]
                    potential.append(value)
                near, far, third = o[0, p, s], o[1, p, s], o[2, p, s]
                u_out[p, s] = -(potential[1] * far)
                far_out[p, s] = -(potential[0] * near + potential[1] * third)
                near_out[p, s] = -(potential[0] * far)
        part = pl.ds(t * step, step)
        remote(far_out.at[part], out.at[0, pl.ds(chunk * step, step), pl.ds(height * y, height)],
               out_s.at[1, h, chunk], out_r.at[1, yl, chunk], device(x, 1 - yh, z, core, h)).start()
        remote(u_out.at[part], u_in.at[part], u_s.at[h, chunk], u_r.at[h, chunk],
               device(x + dx, yh, z, yl, core)).start()
        return carry

    lax.fori_loop(0, 2 * CHUNKS, finish, 0)

    def finish_near(t, carry):
        h, chunk = t // CHUNKS, lax.rem(t, CHUNKS)
        part = pl.ds(t * step, step)
        arrived(u_in.at[part], u_r.at[h, chunk])
        for i in range(step):
            p = t * step + i
            near_out[p] = near_out[p] + u_in[p]
        either(jnp.logical_and(yl == core, h == core), near_out.at[part],
               out.at[0, pl.ds(chunk * step, step), pl.ds(height * y, height)],
               out_s.at[0, h, chunk], out_r.at[0, yl, chunk], device(x, yh, z, core, h))
        return carry

    lax.fori_loop(0, 2 * CHUNKS, finish_near, 0)

    for side in range(2):
        for l in range(2):
            for chunk in range(CHUNKS):
                whose = flip(yh, 1) if side else yh
                arrived(out.at[0, pl.ds(chunk * step, step), pl.ds(height * (2 * whose + l), height)],
                        out_r.at[side, l, chunk])
    for h in range(2):
        for chunk in range(CHUNKS):
            part = pl.ds(h * half + chunk * step, step)
            sent(far_out.at[part], out_s.at[1, h, chunk])
            sent(u_out.at[part], u_s.at[h, chunk])
            sent(o.at[0, part], third_s.at[h, chunk])

            @pl.when(jnp.logical_not(jnp.logical_and(own, core == h)))
            def _():
                sent(near_out.at[part], out_s.at[0, h, chunk])
    for chunk in range(CHUNKS):
        src = orb.at[0, pl.ds(0, step), pl.ds(0, height)]
        for k in range(1, 4):
            sent(src, near_s.at[k, chunk])

        @pl.when(jnp.logical_not(own))
        def _():
            sent(src, near_s.at[0, chunk])
    block = eps.at[:, pl.ds(0, height)]
    sent(block, eps_s.at[1])

    @pl.when(jnp.logical_not(own))
    def _():
        sent(block, eps_s.at[0])

    for copy in eps_planes:
        copy.wait_send()
    for copy in eps_rows:
        copy.wait_send()
    for gen in range(ITERS):
        for copy in field_planes(gen):
            copy.wait_send()
        for copy in field_rows(gen):
            copy.wait_send()
        for d in range(cz - 1):
            sent(red.at[gen], z_s.at[gen, d])
        for at in range(11):
            sent(yred.at[gen], y_s.at[gen, at])


def per_device(cx, cz, orbitals, dielectric):
    _, deep, width, lanes = orbitals.shape
    planes, height = 2 * deep, width // 4
    full = (planes, height, lanes)
    vmem, dma = pltpu.VMEM, pltpu.SemaphoreType.DMA
    scratch = [
        vmem((3, *full), F32),
        vmem((planes + 2, height, lanes), F32),
        vmem((planes + 1, height, lanes), F32),
        vmem(full, F32),
        vmem(full, F32),
        vmem(full, F32),
        vmem(full, F32),
        vmem((ITERS, 2, planes + 2, height, lanes), F32),
        vmem((ITERS - 1, 2, *full), F32),
        vmem((ITERS, 2, 2, planes, 1, lanes), F32),
        vmem((ITERS, 2, 2, planes, 1, lanes), F32),
        vmem((2, planes, 1, lanes), F32),
        vmem((2, planes, 1, lanes), F32),
        vmem((ITERS, 8, lanes // 2), F32),
        vmem((ITERS, cz - 1, 8, lanes // 2), F32),
        vmem((ITERS, 8, lanes // 2), F32),
        vmem((ITERS, 11, 8, lanes // 2), F32),
        vmem(full, F32),
        vmem(full, F32),
        vmem(full, F32),
        vmem(full, F32),
        dma((4, CHUNKS)),
        dma((3, 2, CHUNKS)),
        dma((2, CHUNKS)),
        dma((2,)),
        dma((2,)),
        dma((ITERS + 1, 2)),
        dma((ITERS + 1, 2)),
        dma((ITERS + 1, 2, 2)),
        dma((ITERS + 1, 2, 2)),
        dma((ITERS, cz - 1)),
        dma((ITERS, cz - 1)),
        dma((ITERS, 11)),
        dma((ITERS, 11)),
        dma((2, 2, CHUNKS)),
        dma((2, 2, CHUNKS)),
        dma((2, CHUNKS)),
        dma((2, CHUNKS)),
    ]
    return pl.pallas_call(
        functools.partial(kernel, cx, cz),
        out_shape=jax.ShapeDtypeStruct(orbitals.shape, F32),
        in_specs=[pl.BlockSpec(memory_space=pl.ANY)] * 2,
        out_specs=pl.BlockSpec(memory_space=pl.ANY),
        scratch_shapes=scratch,
        compiler_params=pltpu.CompilerParams(
            collective_id=0, has_side_effects=True, vmem_limit_bytes=48 * 1024 * 1024
        ),
    )(orbitals, dielectric)


def solution(mesh):
    return jax.shard_map(
        functools.partial(per_device, mesh.shape["blk"] // 2, mesh.shape["dom"] // 4),
        mesh=mesh,
        in_specs=(P("blk", "dom", None, None), P("dom", None, None)),
        out_specs=P("blk", "dom", None, None),
        check_vma=False,
    )
```

```python
import functools
import math

import jax
import jax.numpy as jnp
from jax import lax
from jax.experimental import pallas as pl
from jax.experimental.pallas import tpu as pltpu
from jax.sharding import PartitionSpec as P

FOUR_PI = 4.0 * math.pi
ITERS = 3
SCALE = 1.0 / 16.0
CHUNKS = 4
STRIP = 16
ORDER = (1, 4, 3, 2, 0)
F32 = jnp.float32


def kernel(cx, cz, orb, eps, out, *scratch):
    (o, e, wx, wyp, wym, wzp, wzm, field, pack, rows, epack, erows, red, zin, yred, yin, far_out,
     near_out, u_out, u_in, near_s, near_r, third_s, third_d, eps_s, eps_r, plane_s, plane_r, row_s, row_r, z_s, z_r,
     y_s, y_r, out_s, out_r, u_s, u_r) = scratch
    planes, height, lanes = o.shape[1:]
    half = planes // 2
    step = half // CHUNKS
    blk, dom = lax.axis_index("blk"), lax.axis_index("dom")
    x, yh = blk // 2, blk % 2
    z, yl, core = dom // 4, (dom // 2) % 2, dom % 2
    y = 2 * yh + yl
    dx = 1 - 2 * yh

    def flip(value, by):
        return value + by - 2 * by * value if by else value

    def device(x_, yh_, z_, yl_, core_):
        x_, z_ = lax.rem(x_ + cx, cx), lax.rem(z_ + cz, cz)
        return {"blk": x_ * 2 + yh_, "dom": z_ * 4 + yl_ * 2 + core_}

    def remote(src, dst, send, recv, to):
        return pltpu.make_async_remote_copy(src_ref=src, dst_ref=dst, send_sem=send, recv_sem=recv, device_id=to)

    here = device(x, yh, z, yl, core)

    def arrived(dst, recv):
        pltpu.make_async_copy(dst, dst, recv).wait()

    def sent(src, send):
        pltpu.make_async_copy(src, src, send).wait()

    def either(is_self, src, dst, send, recv, to):
        @pl.when(is_self)
        def _():
            pltpu.make_async_copy(src, dst, recv).start()

        @pl.when(jnp.logical_not(is_self))
        def _():
            remote(src, dst, send, recv, to).start()

    barrier = pltpu.get_barrier_semaphore()
    partners = []
    for k in range(4):
        for cc in range(2):
            if k or cc:
                partners.append(device(x, flip(yh, k // 2), z, flip(yl, k % 2), flip(core, cc)))
    partners += [device(x + 1, yh, z, yl, core), device(x - 1, yh, z, yl, core)]
    partners += [device(x, yh, z + d, yl, core) for d in range(1, cz)]
    partners.append(device(x, yh, z + 2 * core - 1, yl, 1 - core))
    for k in range(2):
        for cc in range(2):
            partners.append(device(x + dx, 1 - yh, z, flip(yl, k), flip(core, cc)))
    own = core == yl
    partners.append(device(x + jnp.where(own, dx, -dx), yh, z, yl, 1 - core))
    for partner in partners:
        pl.semaphore_signal(barrier, inc=1, device_id=partner)
    pl.semaphore_wait(barrier, len(partners))

    y_other = lax.rem(y + 1 + 2 * core, 4)
    e_here = e.at[pl.ds(1 + half * core, half)]
    either(own, eps.at[:, pl.ds(height * y, height)], e_here, eps_s.at[0], eps_r.at[core],
           device(x, yh, z, yl, yl))
    remote(eps.at[:, pl.ds(height * y_other, height)], e_here, eps_s.at[1], eps_r.at[core],
           device(x, y_other // 2, z, lax.rem(y_other, 2), yl)).start()
    for chunk in range(CHUNKS):
        for k in ORDER:
            here_o = pl.ds(half * core + step * chunk, step)
            if k == 4:
                src = orb.at[0, pl.ds(step * chunk, step), pl.ds(height * y, height)]
                remote(src, o.at[2, here_o], third_d.at[chunk], near_r.at[2, core, chunk],
                       device(x - dx, yh, z, yl, yl)).start()
                continue
            jh, jl = flip(yh, k // 2), flip(yl, k % 2)
            src = orb.at[0, pl.ds(step * chunk, step), pl.ds(height * (2 * jh + jl), height)]
            dst = o.at[k // 2, here_o]
            sems = near_s.at[k, chunk], near_r.at[k // 2, core, chunk]
            to = device(x, jh, z, jl, yl)
            if k:
                remote(src, dst, *sems, to).start()
            else:
                either(own, src, dst, *sems, to)

    def relay(t, carry):
        h, chunk = lax.rem(t, 2), t // 2
        part = pl.ds(h * half + chunk * step, step)
        arrived(o.at[0, part], near_r.at[0, h, chunk])

        @pl.when(jnp.logical_not(own))
        def _():
            remote(o.at[0, part], o.at[2, part], third_s.at[h, chunk], near_r.at[2, h, chunk],
                   device(x - dx, yh, z, yl, core)).start()

        return carry

    lax.fori_loop(0, 2 * CHUNKS, relay, 0)

    j_down, j_up = lax.rem(y + 1, 4), lax.rem(y + 3, 4)
    x_down = (x + jnp.where(y == 1, 1, 0), x + jnp.where(y == 1, 1, 0))
    x_up = x - jnp.where(y == 2, 1, 0)
    to_row = (
        (device(x, j_up // 2, z, lax.rem(j_up, 2), core), device(x, j_down // 2, z, lax.rem(j_down, 2), core)),
        (device(x_up, j_up // 2, z, lax.rem(j_up, 2), core),
         device(x_down[1], j_down // 2, z, lax.rem(j_down, 2), core)),
    )
    to_plane = (device(x, yh, z - 1 + core, yl, 1 - core), device(x, yh, z + core, yl, 1 - core))
    first_plane = jnp.logical_and(z == 0, core == 0)
    last_plane = jnp.logical_and(z == cz - 1, core == 1)

    def plane_copies(gen, lower, upper, lower_to, upper_to):
        return (remote(lower, upper_to, plane_s.at[gen, 0], plane_r.at[gen, 0], to_plane[0]),
                remote(upper, lower_to, plane_s.at[gen, 1], plane_r.at[gen, 1], to_plane[1]))

    def field_planes(gen):
        f = field.at[gen]
        return plane_copies(gen, f.at[:, 1], f.at[:, planes], f.at[:, 0], f.at[:, planes + 1])

    def field_rows(gen):
        return [remote(pack.at[gen, job, side], rows.at[gen, job, 1 - side], row_s.at[gen, job, side],
                       row_r.at[gen, job, 1 - side], to_row[job][side]) for job in range(2) for side in range(2)]

    def start(copies):
        for copy in copies:
            copy.start()

    def finish_rows(gen):
        for job in range(2):
            for side in range(2):
                arrived(rows.at[gen, job, side], row_r.at[gen, job, side])
        for side, edge in ((0, y == 0), (1, y == 3)):
            @pl.when(edge)
            def _():
                for job in range(2):
                    rows[gen, job, side] = jnp.zeros(rows.shape[3:], F32)

    def finish_planes(gen):
        f = field.at[gen]
        arrived(f.at[:, planes + 1], plane_r.at[gen, 0])
        arrived(f.at[:, 0], plane_r.at[gen, 1])
        for edge, at in ((first_plane, 0), (last_plane, planes + 1)):
            @pl.when(edge)
            def _():
                for job in range(2):
                    field[gen, job, at] = jnp.zeros((height, lanes), F32)

    def store_rows(gen, job, p, value):
        pack[gen, job, 0, p] = value[0:1]
        pack[gen, job, 1, p] = value[height - 1 : height]

    for h in range(2):
        arrived(e.at[pl.ds(1 + half * h, half)], eps_r.at[h])

    def pack_eps(p, carry):
        epack[0, p] = e[p + 1, 0:1]
        epack[1, p] = e[p + 1, height - 1 : height]
        return carry

    lax.fori_loop(0, planes, pack_eps, 0)
    eps_planes = plane_copies(ITERS, e.at[1], e.at[planes], e.at[0], e.at[planes + 1])
    eps_rows = [remote(epack.at[side], erows.at[1 - side], row_s.at[ITERS, 0, side], row_r.at[ITERS, 0, 1 - side],
                       to_row[0][side]) for side in range(2)]
    start(eps_planes)
    start(eps_rows)
    for side in range(2):
        arrived(erows.at[side], row_r.at[ITERS, 0, side])
    arrived(e.at[planes + 1], plane_r.at[ITERS, 0])
    arrived(e.at[0], plane_r.at[ITERS, 1])
    for edge, at in ((first_plane, 0), (last_plane, planes + 1)):
        @pl.when(edge)
        def _():
            e[at] = jnp.zeros((height, lanes), F32)
    for side, edge in ((0, y == 0), (1, y == 3)):
        @pl.when(edge)
        def _():
            erows[side] = jnp.zeros(erows.shape[1:], F32)

    row_at = lax.broadcasted_iota(jnp.int32, (STRIP, lanes), 0)
    lane_at = lax.broadcasted_iota(jnp.int32, (STRIP, lanes), 1)

    def four(value, before, after):
        below = jnp.where(row_at == STRIP - 1, after, pltpu.roll(value, STRIP - 1, 0))
        above = jnp.where(row_at == 0, before, pltpu.roll(value, 1, 0))
        right = jnp.where(lane_at == lanes - 1, 0.0, pltpu.roll(value, lanes - 1, 1))
        left = jnp.where(lane_at == 0, 0.0, pltpu.roll(value, 1, 1))
        return below, above, right, left

    def weigh(p, carry):
        for r in range(0, height, STRIP):
            s = pl.ds(r, STRIP)
            value = e[p + 1, s]
            before = e[p + 1, r - 1 : r] if r else erows[0, p]
            after = e[p + 1, r + STRIP : r + STRIP + 1] if r + STRIP < height else erows[1, p]
            below, above, right, left = four(value, before, after)
            wyp[p, s] = (value + below) * (0.5 * SCALE)
            wym[p, s] = (value + above) * (0.5 * SCALE)
            wzp[p, s] = (value + right) * (0.5 * SCALE)
            wzm[p, s] = (value + left) * (0.5 * SCALE)
            wx[p, s] = (value + e[p, s]) * (0.5 * SCALE)
        return carry

    lax.fori_loop(0, planes, weigh, 0)
    wx[planes] = (e[planes] + e[planes + 1]) * (0.5 * SCALE)

    def density(t, carry):
        h, chunk = t // CHUNKS, lax.rem(t, CHUNKS)
        part = pl.ds(t * step, step)
        arrived(o.at[1, part], near_r.at[1, h, chunk])
        arrived(o.at[2, part], near_r.at[2, h, chunk])
        for i in range(step):
            p = t * step + i
            far = FOUR_PI * o[1, p]
            for job, other in ((0, 0), (1, 2)):
                value = far * o[other, p]
                field[0, job, p + 1] = value
                store_rows(0, job, p, value)
        return carry

    lax.fori_loop(0, 2 * CHUNKS, density, 0)

    def folded(value):
        total = value[0:8]
        for r in range(8, STRIP, 8):
            total = total + value[r : r + 8]
        return total[:, : lanes // 2] + total[:, lanes // 2 :]

    def apply(gen, strips, p, sums):
        sums = list(sums)
        for r in strips:
            s = pl.ds(r, STRIP)
            for job in range(2):
                value = field[gen, job, p + 1, s]
                before = field[gen, job, p + 1, r - 1 : r] if r else rows[gen, job, 0, p]
                after = field[gen, job, p + 1, r + STRIP : r + STRIP + 1] if r + STRIP < height else rows[gen, job, 1, p]
                below, above, right, left = four(value, before, after)
                result = wx[p + 1, s] * (value - field[gen, job, p + 2, s])
                result += wx[p, s] * (value - field[gen, job, p, s])
                result += wyp[p, s] * (value - below)
                result += wym[p, s] * (value - above)
                result += wzp[p, s] * (value - right)
                result += wzm[p, s] * (value - left)
                if gen < ITERS - 1:
                    field[gen + 1, job, p + 1, s] = result
                    if r == 0:
                        pack[gen + 1, job, 0, p] = result[0:1]
                    if r + STRIP == height:
                        pack[gen + 1, job, 1, p] = result[STRIP - 1 : STRIP]
                sums[2 * job] += folded(value * value)
                sums[2 * job + 1] += folded(value * result)
        return tuple(sums)

    half_lanes = lanes // 2
    tile_row = lax.broadcasted_iota(jnp.int32, (16, half_lanes), 0)
    strips = list(range(0, height, STRIP))

    tile = jnp.zeros((16, half_lanes), F32)
    for gen in range(ITERS):
        start(field_planes(gen))
        start(field_rows(gen))
        sums = (jnp.zeros((8, half_lanes), F32),) * 4
        sums = lax.fori_loop(1, planes - 1, functools.partial(apply, gen, strips[1:-1]), sums)
        finish_rows(gen)
        sums = lax.fori_loop(1, planes - 1, functools.partial(apply, gen, (strips[0], strips[-1])), sums)
        finish_planes(gen)
        sums = lax.fori_loop(0, 2, lambda i, c: apply(gen, strips, i * (planes - 1), c), sums)
        for job in range(2):
            for q in range(2):
                part = jnp.sum(sums[2 * job + q], axis=0, keepdims=True)
                tile = jnp.where(tile_row == 8 * job + 2 * gen + q, part, tile)

    red[...] = tile
    for d in range(1, cz):
        remote(red, zin.at[d - 1], z_s.at[d - 1], z_r.at[d - 1], device(x, yh, z + d, yl, core)).start()
    for d in range(1, cz):
        arrived(zin.at[d - 1], z_r.at[d - 1])
        tile = tile + zin[d - 1]
    yred[...] = tile
    relations = [(x_, h, k, cc) for x_, h in ((0, 0), (0, 1), (1, 1)) for k in range(2) for cc in range(2)][1:]
    for at, (x_, h, k, cc) in enumerate(relations):
        remote(yred, yin.at[at], y_s.at[at], y_r.at[at],
               device(x + dx * x_, flip(yh, h), z, flip(yl, k), flip(core, cc))).start()
    for at, (x_, h, k, cc) in enumerate(relations):
        arrived(yin.at[at], y_r.at[at])
        other = yin[at]
        if h:
            other = jnp.where((tile_row // 8) == x_, other, 0.0)
        tile = tile + other

    total = jnp.broadcast_to(jnp.sum(tile, axis=1, keepdims=True), (16, half_lanes))
    coefficient = []
    for job in range(2):
        m = [total[8 * job + k : 8 * job + k + 1] for k in range(6)]
        m = [value / m[0] for value in m]
        l1, l2 = m[2] / m[1], m[3] / m[1]
        d2, f2 = m[3] - l1 * m[2], m[4] - l2 * m[2]
        l3 = f2 / d2
        d3 = m[5] - l2 * m[3] - l3 * f2
        g1 = m[1] - l1
        c2 = (m[2] - l2 - l3 * g1) / d3
        c1 = g1 / d2 - l3 * c2
        c0 = 1.0 / m[1] - l1 * c1 - l2 * c2
        coefficient.append([(SCALE * c)[0, 0] for c in (c0, c1, c2)])

    def finish(t, carry):
        h, chunk = t // CHUNKS, lax.rem(t, CHUNKS)
        for i in range(step):
            p = t * step + i
            for r in range(0, height, 2 * STRIP):
                s = pl.ds(r, 2 * STRIP)
                potential = []
                for job in range(2):
                    value = coefficient[job][0] * field[0, job, p + 1, s]
                    for gen in range(1, ITERS):
                        value = value + coefficient[job][gen] * field[gen, job, p + 1, s]
                    potential.append(value)
                near, far, third = o[0, p, s], o[1, p, s], o[2, p, s]
                u_out[p, s] = -(potential[1] * far)
                far_out[p, s] = -(potential[0] * near + potential[1] * third)
                near_out[p, s] = -(potential[0] * far)
        part = pl.ds(t * step, step)
        remote(far_out.at[part], out.at[0, pl.ds(chunk * step, step), pl.ds(height * y, height)],
               out_s.at[1, h, chunk], out_r.at[1, yl, chunk], device(x, 1 - yh, z, core, h)).start()
        remote(u_out.at[part], u_in.at[part], u_s.at[h, chunk], u_r.at[h, chunk],
               device(x + dx, yh, z, yl, core)).start()
        return carry

    lax.fori_loop(0, 2 * CHUNKS, finish, 0)

    def finish_near(t, carry):
        h, chunk = t // CHUNKS, lax.rem(t, CHUNKS)
        part = pl.ds(t * step, step)
        arrived(u_in.at[part], u_r.at[h, chunk])
        for i in range(step):
            p = t * step + i
            near_out[p] = near_out[p] + u_in[p]
        either(jnp.logical_and(yl == core, h == core), near_out.at[part],
               out.at[0, pl.ds(chunk * step, step), pl.ds(height * y, height)],
               out_s.at[0, h, chunk], out_r.at[0, yl, chunk], device(x, yh, z, core, h))
        return carry

    lax.fori_loop(0, 2 * CHUNKS, finish_near, 0)

    for side in range(2):
        for l in range(2):
            for chunk in range(CHUNKS):
                whose = flip(yh, 1) if side else yh
                arrived(out.at[0, pl.ds(chunk * step, step), pl.ds(height * (2 * whose + l), height)],
                        out_r.at[side, l, chunk])
    for h in range(2):
        for chunk in range(CHUNKS):
            part = pl.ds(h * half + chunk * step, step)
            sent(far_out.at[part], out_s.at[1, h, chunk])
            sent(u_out.at[part], u_s.at[h, chunk])

            @pl.when(jnp.logical_not(own))
            def _():
                sent(o.at[0, part], third_s.at[h, chunk])

            @pl.when(jnp.logical_not(jnp.logical_and(own, core == h)))
            def _():
                sent(near_out.at[part], out_s.at[0, h, chunk])
    for chunk in range(CHUNKS):
        src = orb.at[0, pl.ds(0, step), pl.ds(0, height)]
        for k in range(1, 4):
            sent(src, near_s.at[k, chunk])
        sent(src, third_d.at[chunk])

        @pl.when(jnp.logical_not(own))
        def _():
            sent(src, near_s.at[0, chunk])
    block = eps.at[:, pl.ds(0, height)]
    sent(block, eps_s.at[1])

    @pl.when(jnp.logical_not(own))
    def _():
        sent(block, eps_s.at[0])

    for copy in eps_planes:
        copy.wait_send()
    for copy in eps_rows:
        copy.wait_send()
    for gen in range(ITERS):
        for copy in field_planes(gen):
            copy.wait_send()
        for copy in field_rows(gen):
            copy.wait_send()
    for d in range(cz - 1):
        sent(red, z_s.at[d])
    for at in range(11):
        sent(yred, y_s.at[at])


def per_device(cx, cz, orbitals, dielectric):
    _, deep, width, lanes = orbitals.shape
    planes, height = 2 * deep, width // 4
    full = (planes, height, lanes)
    vmem, dma = pltpu.VMEM, pltpu.SemaphoreType.DMA
    scratch = [
        vmem((3, *full), F32),
        vmem((planes + 2, height, lanes), F32),
        vmem((planes + 1, height, lanes), F32),
        vmem(full, F32),
        vmem(full, F32),
        vmem(full, F32),
        vmem(full, F32),
        vmem((ITERS, 2, planes + 2, height, lanes), F32),
        vmem((ITERS, 2, 2, planes, 1, lanes), F32),
        vmem((ITERS, 2, 2, planes, 1, lanes), F32),
        vmem((2, planes, 1, lanes), F32),
        vmem((2, planes, 1, lanes), F32),
        vmem((16, lanes // 2), F32),
        vmem((cz - 1, 16, lanes // 2), F32),
        vmem((16, lanes // 2), F32),
        vmem((11, 16, lanes // 2), F32),
        vmem(full, F32),
        vmem(full, F32),
        vmem(full, F32),
        vmem(full, F32),
        dma((4, CHUNKS)),
        dma((3, 2, CHUNKS)),
        dma((2, CHUNKS)),
        dma((CHUNKS,)),
        dma((2,)),
        dma((2,)),
        dma((ITERS + 1, 2)),
        dma((ITERS + 1, 2)),
        dma((ITERS + 1, 2, 2)),
        dma((ITERS + 1, 2, 2)),
        dma((cz - 1,)),
        dma((cz - 1,)),
        dma((11,)),
        dma((11,)),
        dma((2, 2, CHUNKS)),
        dma((2, 2, CHUNKS)),
        dma((2, CHUNKS)),
        dma((2, CHUNKS)),
    ]
    return pl.pallas_call(
        functools.partial(kernel, cx, cz),
        out_shape=jax.ShapeDtypeStruct(orbitals.shape, F32),
        in_specs=[pl.BlockSpec(memory_space=pl.ANY)] * 2,
        out_specs=pl.BlockSpec(memory_space=pl.ANY),
        scratch_shapes=scratch,
        compiler_params=pltpu.CompilerParams(
            collective_id=0, has_side_effects=True, vmem_limit_bytes=60 * 1024 * 1024
        ),
    )(orbitals, dielectric)


def solution(mesh):
    return jax.shard_map(
        functools.partial(per_device, mesh.shape["blk"] // 2, mesh.shape["dom"] // 4),
        mesh=mesh,
        in_specs=(P("blk", "dom", None, None), P("dom", None, None)),
        out_specs=P("blk", "dom", None, None),
        check_vma=False,
    )
```

```python
import functools
import math

import jax
import jax.numpy as jnp
from jax import lax
from jax.experimental import pallas as pl
from jax.experimental.pallas import tpu as pltpu
from jax.sharding import PartitionSpec as P

FOUR_PI = 4.0 * math.pi
ITERS = 3
SCALE = 1.0 / 16.0
CHUNKS = 4
AHEAD = 2
SEQUENCE = (0, 3, 1, 2)
STRIP = 16
F32 = jnp.float32


def kernel(cx, cz, orb, eps, out, *scratch):
    (o, e, eblock, wx, wyp, wym, wzp, wzm, field, pack, rows, erows, red, zin, yred, yin, far_out, near_out, u_out, u_in,
     own_s, far_s, far_r, third_s, third_r, eps_s, plane_s, plane_r, row_s, row_r, z_s, z_r, y_s, y_r, near_s, out_s,
     out_r, u_s, u_r) = scratch
    planes, height, lanes = o.shape[1:]
    step = planes // CHUNKS
    blk, dom = lax.axis_index("blk"), lax.axis_index("dom")
    x, yh = blk // 2, blk % 2
    z, yl, core = dom // 4, (dom // 2) % 2, dom % 2
    dx = 1 - 2 * yh

    def flip(value, by):
        return value + by - 2 * by * value if by else value

    def device(x_, yh_, z_, yl_, core_):
        x_, z_ = lax.rem(x_ + cx, cx), lax.rem(z_ + cz, cz)
        return {"blk": x_ * 2 + yh_, "dom": z_ * 4 + yl_ * 2 + core_}

    def remote(src, dst, send, recv, to):
        return pltpu.make_async_remote_copy(src_ref=src, dst_ref=dst, send_sem=send, recv_sem=recv, device_id=to)

    def arrived(dst, recv):
        pltpu.make_async_copy(dst, dst, recv).wait()

    def sent(src, send):
        pltpu.make_async_copy(src, src, send).wait()

    barrier = pltpu.get_barrier_semaphore()
    partners = []
    for k in range(4):
        for cc in range(2):
            if k or cc:
                partners.append(device(x, flip(yh, k // 2), z, flip(yl, k % 2), flip(core, cc)))
    partners += [device(x + 1, yh, z, yl, core), device(x - 1, yh, z, yl, core)]
    partners += [device(x, yh, z + d, yl, core) for d in range(1, cz)]
    below, above = lax.rem(dom + 4 * cz - 1, 4 * cz), lax.rem(dom + 1, 4 * cz)
    to_plane = {"blk": blk, "dom": below}, {"blk": blk, "dom": above}
    partners += to_plane
    for k in range(2):
        for cc in range(2):
            partners.append(device(x + dx, 1 - yh, z, flip(yl, k), flip(core, cc)))
    for partner in partners:
        pl.semaphore_signal(barrier, inc=1, device_id=partner)
    pl.semaphore_wait(barrier, len(partners))

    across, aside, back = device(x, 1 - yh, z, yl, core), device(x + dx, yh, z, yl, core), device(x - dx, yh, z, yl, core)
    mine, theirs = pl.ds(height * yh, height), pl.ds(height * (1 - yh), height)

    def part(chunk):
        return pl.ds(chunk * step, step)

    def send(chunk):
        remote(orb.at[0, part(chunk), theirs], o.at[1, part(chunk)], far_s.at[chunk], far_r.at[chunk], across).start()
        remote(orb.at[0, part(chunk), mine], o.at[2, part(chunk)], third_s.at[chunk], third_r.at[chunk], back).start()

    for chunk in SEQUENCE[:AHEAD]:
        send(chunk)
    local = [
        pltpu.make_async_copy(eps.at[:, mine], e.at[pl.ds(1, planes)], eps_s.at[0]),
        pltpu.make_async_copy(eps.at[:, pl.ds(height - 8 * yh, 8)], eblock, eps_s.at[1]),
        pltpu.make_async_copy(orb.at[0, :, mine], o.at[0], own_s),
    ]
    for copy in local:
        copy.start()

    to_row = across, device(x + dx, 1 - yh, z, yl, core)
    first_plane, last_plane = dom == 0, dom == 4 * cz - 1
    has_after = jnp.where(yh == 0, 1.0, 0.0)
    has_before = 1.0 - has_after

    def plane_copies(gen, job, lower, upper, lower_to, upper_to):
        return [remote(lower, upper_to, plane_s.at[gen, job, 0], plane_r.at[gen, job, 0], to_plane[0]),
                remote(upper, lower_to, plane_s.at[gen, job, 1], plane_r.at[gen, job, 1], to_plane[1])]

    def halo_planes(gen, job):
        f = field.at[gen, job]
        return plane_copies(gen, job, f.at[1], f.at[planes], f.at[0], f.at[planes + 1])

    def halo_rows(gen, job):
        return [remote(pack.at[gen, job], rows.at[gen, job], row_s.at[gen, job], row_r.at[gen, job], to_row[job])]

    def start(copies):
        for copy in copies:
            copy.start()

    def finish_planes(gen, job):
        for side, edge, at in ((0, last_plane, planes + 1), (1, first_plane, 0)):
            arrived(field.at[gen, job, at], plane_r.at[gen, job, side])

            @pl.when(edge)
            def _():
                field[gen, job, at] = jnp.zeros((height, lanes), F32)

    local[0].wait()
    eps_planes = plane_copies(ITERS, 0, e.at[1], e.at[planes], e.at[0], e.at[planes + 1])
    start(eps_planes)
    local[1].wait()
    erows[0] = eblock[:, 7:8] * has_before
    erows[1] = eblock[:, 0:1] * has_after
    for side, edge, at in ((0, last_plane, planes + 1), (1, first_plane, 0)):
        arrived(e.at[at], plane_r.at[ITERS, 0, side])

        @pl.when(edge)
        def _():
            e[at] = jnp.zeros((height, lanes), F32)

    row_at = lax.broadcasted_iota(jnp.int32, (STRIP, lanes), 0)
    lane_at = lax.broadcasted_iota(jnp.int32, (STRIP, lanes), 1)

    def four(value, before, after):
        below = jnp.where(row_at == STRIP - 1, after, pltpu.roll(value, STRIP - 1, 0))
        above = jnp.where(row_at == 0, before, pltpu.roll(value, 1, 0))
        right = jnp.where(lane_at == lanes - 1, 0.0, pltpu.roll(value, lanes - 1, 1))
        left = jnp.where(lane_at == 0, 0.0, pltpu.roll(value, 1, 1))
        return below, above, right, left

    def weigh(p, carry):
        for r in range(0, height, STRIP):
            s = pl.ds(r, STRIP)
            value = e[p + 1, s]
            before = e[p + 1, r - 1 : r] if r else erows[0, p]
            after = e[p + 1, r + STRIP : r + STRIP + 1] if r + STRIP < height else erows[1, p]
            below, above, right, left = four(value, before, after)
            wyp[p, s] = (value + below) * (0.5 * SCALE)
            wym[p, s] = (value + above) * (0.5 * SCALE)
            wzp[p, s] = (value + right) * (0.5 * SCALE)
            wzm[p, s] = (value + left) * (0.5 * SCALE)
            wx[p, s] = (value + e[p, s]) * (0.5 * SCALE)
        return carry

    lax.fori_loop(0, planes, weigh, 0)
    wx[planes] = (e[planes] + e[planes + 1]) * (0.5 * SCALE)
    local[2].wait()

    def density(job, chunk):
        for i in range(step):
            p = chunk * step + i
            value = FOUR_PI * o[1, p] * o[2 * job, p]
            field[0, job, p + 1] = value
            pack[0, job, p] = value[height - 1 : height] * has_after + value[0:1] * has_before

    for n, chunk in enumerate(SEQUENCE):
        arrived(o.at[1, part(chunk)], far_r.at[chunk])
        if n + AHEAD < CHUNKS:
            send(SEQUENCE[n + AHEAD])
        density(0, chunk)
        if n == 1:
            start(halo_planes(0, 0))
        arrived(o.at[2, part(chunk)], third_r.at[chunk])
        density(1, chunk)
        if n == 1:
            start(halo_planes(0, 1))
    for job in range(2):
        start(halo_rows(0, job))

    def folded(value):
        total = value[0:8]
        for r in range(8, STRIP, 8):
            total = total + value[r : r + 8]
        return total[:, : lanes // 2] + total[:, lanes // 2 :]

    def apply(gen, job, strips, p, sums):
        first_sum, second_sum = sums
        for r in strips:
            s = pl.ds(r, STRIP)
            value = field[gen, job, p + 1, s]
            before = field[gen, job, p + 1, r - 1 : r] if r else rows[gen, job, p] * has_before
            last = r + STRIP == height
            after = rows[gen, job, p] * has_after if last else field[gen, job, p + 1, r + STRIP : r + STRIP + 1]
            below, above, right, left = four(value, before, after)
            result = wx[p + 1, s] * (value - field[gen, job, p + 2, s])
            result += wx[p, s] * (value - field[gen, job, p, s])
            result += wyp[p, s] * (value - below)
            result += wym[p, s] * (value - above)
            result += wzp[p, s] * (value - right)
            result += wzm[p, s] * (value - left)
            if gen < ITERS - 1:
                field[gen + 1, job, p + 1, s] = result
                if r == 0:
                    pack[gen + 1, job, p] = result[0:1] * has_before
                if last:
                    pack[gen + 1, job, p] += result[STRIP - 1 : STRIP] * has_after
            first_sum += folded(value * value)
            second_sum += folded(value * result)
        return first_sum, second_sum

    half_lanes = lanes // 2
    tile_row = lax.broadcasted_iota(jnp.int32, (16, half_lanes), 0)
    strips = list(range(0, height, STRIP))

    tile = jnp.zeros((16, half_lanes), F32)

    def power(gen, job, tile):
        sums = (jnp.zeros((8, half_lanes), F32),) * 2
        sums = lax.fori_loop(1, planes - 1, functools.partial(apply, gen, job, strips[1:-1]), sums)
        arrived(rows.at[gen, job], row_r.at[gen, job])
        sums = lax.fori_loop(1, planes - 1, functools.partial(apply, gen, job, (strips[0], strips[-1])), sums)
        finish_planes(gen, job)
        sums = lax.fori_loop(0, 2, lambda i, c: apply(gen, job, strips, i * (planes - 1), c), sums)
        if gen < ITERS - 1:
            start(halo_planes(gen + 1, job))
            start(halo_rows(gen + 1, job))
        for q in range(2):
            moment = jnp.sum(sums[q], axis=0, keepdims=True)
            tile = jnp.where(tile_row == 8 * job + 2 * gen + q, moment, tile)
        return tile

    for gen in range(ITERS):
        for job in range(2):
            tile = power(gen, job, tile)

    red[...] = tile
    for d in range(1, cz):
        remote(red, zin.at[d - 1], z_s.at[d - 1], z_r.at[d - 1], device(x, yh, z + d, yl, core)).start()
    for d in range(1, cz):
        arrived(zin.at[d - 1], z_r.at[d - 1])
        tile = tile + zin[d - 1]
    yred[...] = tile
    relations = [(x_, h, k, cc) for x_, h in ((0, 0), (0, 1), (1, 1)) for k in range(2) for cc in range(2)][1:]
    for at, (x_, h, k, cc) in enumerate(relations):
        remote(yred, yin.at[at], y_s.at[at], y_r.at[at],
               device(x + dx * x_, flip(yh, h), z, flip(yl, k), flip(core, cc))).start()
    for at, (x_, h, k, cc) in enumerate(relations):
        arrived(yin.at[at], y_r.at[at])
        other = yin[at]
        if h:
            other = jnp.where((tile_row // 8) == x_, other, 0.0)
        tile = tile + other

    total = jnp.broadcast_to(jnp.sum(tile, axis=1, keepdims=True), (16, half_lanes))
    coefficient = []
    for job in range(2):
        m = [jnp.broadcast_to(total[8 * job + k : 8 * job + k + 1], (8, half_lanes)) for k in range(6)]
        i1 = 1.0 / m[1]
        l1, l2 = m[2] * i1, m[3] * i1
        d2, f2 = m[3] - l1 * m[2], m[4] - l2 * m[2]
        i2 = 1.0 / d2
        l3 = f2 * i2
        d3 = m[5] - l2 * m[3] - l3 * f2
        g1 = m[1] - l1 * m[0]
        c2 = (m[2] - l2 * m[0] - l3 * g1) / d3
        c1 = g1 * i2 - l3 * c2
        c0 = m[0] * i1 - l1 * c1 - l2 * c2
        coefficient.append([jnp.concatenate([SCALE * c, SCALE * c], axis=1) for c in (c0, c1, c2)])

    def finish(chunk, carry):
        for i in range(step):
            p = chunk * step + i
            for r in range(0, height, 8):
                s = pl.ds(r, 8)
                potential = []
                for job in range(2):
                    value = coefficient[job][0] * field[0, job, p + 1, s]
                    for gen in range(1, ITERS):
                        value = value + coefficient[job][gen] * field[gen, job, p + 1, s]
                    potential.append(value)
                near, far, third = o[0, p, s], o[1, p, s], o[2, p, s]
                u_out[p, s] = -(potential[1] * far)
                far_out[p, s] = -(potential[0] * near + potential[1] * third)
                near_out[p, s] = -(potential[0] * far)
        remote(far_out.at[part(chunk)], out.at[0, part(chunk), mine], out_s.at[chunk], out_r.at[chunk], across).start()
        remote(u_out.at[part(chunk)], u_in.at[part(chunk)], u_s.at[chunk], u_r.at[chunk], aside).start()
        return carry

    lax.fori_loop(0, CHUNKS, finish, 0)

    def near_copy(chunk):
        return pltpu.make_async_copy(near_out.at[part(chunk)], out.at[0, part(chunk), mine], near_s.at[chunk])

    def finish_near(chunk, carry):
        arrived(u_in.at[part(chunk)], u_r.at[chunk])
        for i in range(step):
            p = chunk * step + i
            near_out[p] = near_out[p] + u_in[p]
        near_copy(chunk).start()
        return carry

    lax.fori_loop(0, CHUNKS, finish_near, 0)

    for chunk in range(CHUNKS):
        arrived(out.at[0, part(chunk), theirs], out_r.at[chunk])
        near_copy(chunk).wait()
        sent(far_out.at[part(chunk)], out_s.at[chunk])
        sent(u_out.at[part(chunk)], u_s.at[chunk])
        sent(orb.at[0, part(chunk), theirs], far_s.at[chunk])
        sent(orb.at[0, part(chunk), mine], third_s.at[chunk])
    for copy in eps_planes:
        copy.wait_send()
    for gen in range(ITERS):
        for job in range(2):
            for copy in halo_planes(gen, job) + halo_rows(gen, job):
                copy.wait_send()
    for d in range(cz - 1):
        sent(red, z_s.at[d])
    for at in range(11):
        sent(yred, y_s.at[at])


def per_device(cx, cz, orbitals, dielectric):
    _, deep, width, lanes = orbitals.shape
    planes, height = deep, width // 2
    full = (planes, height, lanes)
    vmem, dma = pltpu.VMEM, pltpu.SemaphoreType.DMA
    scratch = [
        vmem((3, *full), F32),
        vmem((planes + 2, height, lanes), F32),
        vmem((planes, 8, lanes), F32),
        vmem((planes + 1, height, lanes), F32),
        vmem(full, F32),
        vmem(full, F32),
        vmem(full, F32),
        vmem(full, F32),
        vmem((ITERS, 2, planes + 2, height, lanes), F32),
        vmem((ITERS, 2, planes, 1, lanes), F32),
        vmem((ITERS, 2, planes, 1, lanes), F32),
        vmem((2, planes, 1, lanes), F32),
        vmem((16, lanes // 2), F32),
        vmem((cz - 1, 16, lanes // 2), F32),
        vmem((16, lanes // 2), F32),
        vmem((11, 16, lanes // 2), F32),
        vmem(full, F32),
        vmem(full, F32),
        vmem(full, F32),
        vmem(full, F32),
        dma,
        *[dma((CHUNKS,))] * 4,
        dma((2,)),
        *[dma((ITERS + 1, 2, 2))] * 2,
        *[dma((ITERS, 2))] * 2,
        *[dma((cz - 1,))] * 2,
        *[dma((11,))] * 2,
        *[dma((CHUNKS,))] * 5,
    ]
    return pl.pallas_call(
        functools.partial(kernel, cx, cz),
        out_shape=jax.ShapeDtypeStruct(orbitals.shape, F32),
        in_specs=[pl.BlockSpec(memory_space=pl.ANY)] * 2,
        out_specs=pl.BlockSpec(memory_space=pl.ANY),
        scratch_shapes=scratch,
        compiler_params=pltpu.CompilerParams(
            collective_id=0, has_side_effects=True, vmem_limit_bytes=60 * 1024 * 1024
        ),
    )(orbitals, dielectric)


def solution(mesh):
    return jax.shard_map(
        functools.partial(per_device, mesh.shape["blk"] // 2, mesh.shape["dom"] // 4),
        mesh=mesh,
        in_specs=(P("blk", "dom", None, None), P("dom", None, None)),
        out_specs=P("blk", "dom", None, None),
        check_vma=False,
    )
```

```python
import functools
import math

import jax
import jax.numpy as jnp
from jax import lax
from jax.experimental import pallas as pl
from jax.experimental.pallas import tpu as pltpu
from jax.sharding import PartitionSpec as P

FOUR_PI = 4.0 * math.pi
ITERS = 3
SCALE = 1.0 / 16.0
CHUNKS = 4
AHEAD = 2
SEQUENCE = (0, 3, 1, 2)
STRIP = 16
F32 = jnp.float32


def kernel(cx, cz, orb, eps, out, *scratch):
    (o, e, eblock, wx, wyp, wym, wzp, wzm, field, pack, rows, erows, red, zin, yred, yin, far_out, near_out, u_out, u_in,
     own_s, far_s, far_r, third_s, third_r, eps_s, plane_s, plane_r, row_s, row_r, z_s, z_r, y_s, y_r, near_s, out_s,
     out_r, u_s, u_r) = scratch
    planes, height, lanes = o.shape[1:]
    step = planes // CHUNKS
    blk, dom = lax.axis_index("blk"), lax.axis_index("dom")
    x, yh = blk // 2, blk % 2
    z, yl, core = dom // 4, (dom // 2) % 2, dom % 2
    dx = 1 - 2 * yh

    def flip(value, by):
        return value + by - 2 * by * value if by else value

    def device(x_, yh_, z_, yl_, core_):
        x_, z_ = lax.rem(x_ + cx, cx), lax.rem(z_ + cz, cz)
        return {"blk": x_ * 2 + yh_, "dom": z_ * 4 + yl_ * 2 + core_}

    def remote(src, dst, send, recv, to):
        return pltpu.make_async_remote_copy(src_ref=src, dst_ref=dst, send_sem=send, recv_sem=recv, device_id=to)

    def arrived(dst, recv):
        pltpu.make_async_copy(dst, dst, recv).wait()

    def sent(src, send):
        pltpu.make_async_copy(src, src, send).wait()

    barrier = pltpu.get_barrier_semaphore()
    partners = []
    for k in range(4):
        for cc in range(2):
            if k or cc:
                partners.append(device(x, flip(yh, k // 2), z, flip(yl, k % 2), flip(core, cc)))
    partners += [device(x + 1, yh, z, yl, core), device(x - 1, yh, z, yl, core)]
    partners += [device(x, yh, z + d, yl, core) for d in range(1, cz)]
    below, above = lax.rem(dom + 4 * cz - 1, 4 * cz), lax.rem(dom + 1, 4 * cz)
    to_plane = {"blk": blk, "dom": below}, {"blk": blk, "dom": above}
    partners += to_plane
    for k in range(2):
        for cc in range(2):
            partners.append(device(x + dx, 1 - yh, z, flip(yl, k), flip(core, cc)))
    for partner in partners:
        pl.semaphore_signal(barrier, inc=1, device_id=partner)
    pl.semaphore_wait(barrier, len(partners))

    across, aside, back = device(x, 1 - yh, z, yl, core), device(x + dx, yh, z, yl, core), device(x - dx, yh, z, yl, core)
    mine, theirs = pl.ds(height * yh, height), pl.ds(height * (1 - yh), height)

    def part(chunk):
        return pl.ds(chunk * step, step)

    def send(chunk):
        remote(orb.at[0, part(chunk), theirs], o.at[1, part(chunk)], far_s.at[chunk], far_r.at[chunk], across).start()
        remote(orb.at[0, part(chunk), mine], o.at[2, part(chunk)], third_s.at[chunk], third_r.at[chunk], back).start()

    for chunk in SEQUENCE[:AHEAD]:
        send(chunk)
    local = [
        pltpu.make_async_copy(eps.at[:, mine], e.at[pl.ds(1, planes)], eps_s.at[0]),
        pltpu.make_async_copy(eps.at[:, pl.ds(height - 8 * yh, 8)], eblock, eps_s.at[1]),
        pltpu.make_async_copy(orb.at[0, :, mine], o.at[0], own_s),
    ]
    for copy in local:
        copy.start()

    to_row = across, device(x + dx, 1 - yh, z, yl, core)
    first_plane, last_plane = dom == 0, dom == 4 * cz - 1
    has_after = jnp.where(yh == 0, 1.0, 0.0)
    has_before = 1.0 - has_after

    def plane_copies(gen, job, lower, upper, lower_to, upper_to):
        return [remote(lower, upper_to, plane_s.at[gen, job, 0], plane_r.at[gen, job, 0], to_plane[0]),
                remote(upper, lower_to, plane_s.at[gen, job, 1], plane_r.at[gen, job, 1], to_plane[1])]

    def halo_planes(gen, job):
        f = field.at[gen, job]
        return plane_copies(gen, job, f.at[1], f.at[planes], f.at[0], f.at[planes + 1])

    def halo_rows(gen, job):
        return [remote(pack.at[gen, job], rows.at[gen, job], row_s.at[gen, job], row_r.at[gen, job], to_row[job])]

    def start(copies):
        for copy in copies:
            copy.start()

    def finish_planes(gen, job):
        for side, edge, at in ((0, last_plane, planes + 1), (1, first_plane, 0)):
            arrived(field.at[gen, job, at], plane_r.at[gen, job, side])

            @pl.when(edge)
            def _():
                field[gen, job, at] = jnp.zeros((height, lanes), F32)

    local[0].wait()
    eps_planes = plane_copies(ITERS, 0, e.at[1], e.at[planes], e.at[0], e.at[planes + 1])
    start(eps_planes)
    local[1].wait()
    erows[0] = eblock[:, 7:8] * has_before
    erows[1] = eblock[:, 0:1] * has_after
    for side, edge, at in ((0, last_plane, planes + 1), (1, first_plane, 0)):
        arrived(e.at[at], plane_r.at[ITERS, 0, side])

        @pl.when(edge)
        def _():
            e[at] = jnp.zeros((height, lanes), F32)

    row_at = lax.broadcasted_iota(jnp.int32, (STRIP, lanes), 0)
    lane_at = lax.broadcasted_iota(jnp.int32, (STRIP, lanes), 1)

    def four(value, before, after):
        below = jnp.where(row_at == STRIP - 1, after, pltpu.roll(value, STRIP - 1, 0))
        above = jnp.where(row_at == 0, before, pltpu.roll(value, 1, 0))
        right = jnp.where(lane_at == lanes - 1, 0.0, pltpu.roll(value, lanes - 1, 1))
        left = jnp.where(lane_at == 0, 0.0, pltpu.roll(value, 1, 1))
        return below, above, right, left

    def weigh(p, carry):
        for r in range(0, height, STRIP):
            s = pl.ds(r, STRIP)
            value = e[p + 1, s]
            before = e[p + 1, r - 1 : r] if r else erows[0, p]
            after = e[p + 1, r + STRIP : r + STRIP + 1] if r + STRIP < height else erows[1, p]
            below, above, right, left = four(value, before, after)
            wyp[p, s] = (value + below) * (0.5 * SCALE)
            wym[p, s] = (value + above) * (0.5 * SCALE)
            wzp[p, s] = (value + right) * (0.5 * SCALE)
            wzm[p, s] = (value + left) * (0.5 * SCALE)
            wx[p, s] = (value + e[p, s]) * (0.5 * SCALE)
        return carry

    lax.fori_loop(0, planes, weigh, 0)
    wx[planes] = (e[planes] + e[planes + 1]) * (0.5 * SCALE)
    local[2].wait()

    def density(job, chunk):
        for i in range(step):
            p = chunk * step + i
            value = FOUR_PI * o[1, p] * o[2 * job, p]
            field[0, job, p + 1] = value
            pack[0, job, p] = value[height - 1 : height] * has_after + value[0:1] * has_before

    def second_density(n, chunk):
        arrived(o.at[2, part(chunk)], third_r.at[chunk])
        density(1, chunk)
        if n == 1:
            start(halo_planes(0, 1))

    for n, chunk in enumerate(SEQUENCE):
        arrived(o.at[1, part(chunk)], far_r.at[chunk])
        if n + AHEAD < CHUNKS:
            send(SEQUENCE[n + AHEAD])
        density(0, chunk)
        if n == 1:
            start(halo_planes(0, 0))
        if n < CHUNKS - 1:
            second_density(n, chunk)

    start(halo_rows(0, 0))

    def folded(value):
        total = value[0:8]
        for r in range(8, STRIP, 8):
            total = total + value[r : r + 8]
        return total[:, : lanes // 2] + total[:, lanes // 2 :]

    def apply(gen, job, strips, p, sums):
        first_sum, second_sum = sums
        for r in strips:
            s = pl.ds(r, STRIP)
            value = field[gen, job, p + 1, s]
            before = field[gen, job, p + 1, r - 1 : r] if r else rows[gen, job, p] * has_before
            last = r + STRIP == height
            after = rows[gen, job, p] * has_after if last else field[gen, job, p + 1, r + STRIP : r + STRIP + 1]
            below, above, right, left = four(value, before, after)
            result = wx[p + 1, s] * (value - field[gen, job, p + 2, s])
            result += wx[p, s] * (value - field[gen, job, p, s])
            result += wyp[p, s] * (value - below)
            result += wym[p, s] * (value - above)
            result += wzp[p, s] * (value - right)
            result += wzm[p, s] * (value - left)
            if gen < ITERS - 1:
                field[gen + 1, job, p + 1, s] = result
                if r == 0:
                    pack[gen + 1, job, p] = result[0:1] * has_before
                if last:
                    pack[gen + 1, job, p] += result[STRIP - 1 : STRIP] * has_after
            first_sum += folded(value * value)
            second_sum += folded(value * result)
        return first_sum, second_sum

    half_lanes = lanes // 2
    tile_row = lax.broadcasted_iota(jnp.int32, (16, half_lanes), 0)
    strips = list(range(0, height, STRIP))

    tile = jnp.zeros((16, half_lanes), F32)

    def power(gen, job, tile):
        sums = (jnp.zeros((8, half_lanes), F32),) * 2
        sums = lax.fori_loop(1, planes - 1, functools.partial(apply, gen, job, strips[1:-1]), sums)
        if gen == job == 0:
            second_density(CHUNKS - 1, SEQUENCE[-1])
            start(halo_rows(0, 1))
        arrived(rows.at[gen, job], row_r.at[gen, job])
        sums = lax.fori_loop(1, planes - 1, functools.partial(apply, gen, job, (strips[0], strips[-1])), sums)
        finish_planes(gen, job)
        sums = lax.fori_loop(0, 2, lambda i, c: apply(gen, job, strips, i * (planes - 1), c), sums)
        if gen < ITERS - 1:
            start(halo_planes(gen + 1, job))
            start(halo_rows(gen + 1, job))
        for q in range(2):
            moment = jnp.sum(sums[q], axis=0, keepdims=True)
            tile = jnp.where(tile_row == 8 * job + 2 * gen + q, moment, tile)
        return tile

    for gen in range(ITERS):
        for job in range(2):
            tile = power(gen, job, tile)

    red[...] = tile
    for d in sorted(range(1, cz), key=lambda d: -min(d, cz - d)):
        remote(red, zin.at[d - 1], z_s.at[d - 1], z_r.at[d - 1], device(x, yh, z + d, yl, core)).start()
    for d in range(1, cz):
        arrived(zin.at[d - 1], z_r.at[d - 1])
        tile = tile + zin[d - 1]
    yred[...] = tile
    relations = [(x_, h, k, cc) for x_, h in ((0, 0), (0, 1), (1, 1)) for k in range(2) for cc in range(2)][1:]
    for at, (x_, h, k, cc) in reversed(list(enumerate(relations))):
        remote(yred, yin.at[at], y_s.at[at], y_r.at[at],
               device(x + dx * x_, flip(yh, h), z, flip(yl, k), flip(core, cc))).start()
    for at, (x_, h, k, cc) in enumerate(relations):
        arrived(yin.at[at], y_r.at[at])
        other = yin[at]
        if h:
            other = jnp.where((tile_row // 8) == x_, other, 0.0)
        tile = tile + other

    total = jnp.broadcast_to(jnp.sum(tile, axis=1, keepdims=True), (16, half_lanes))
    coefficient = []
    for job in range(2):
        m = [jnp.broadcast_to(total[8 * job + k : 8 * job + k + 1], (8, half_lanes)) for k in range(6)]
        i1 = 1.0 / m[1]
        l1, l2 = m[2] * i1, m[3] * i1
        d2, f2 = m[3] - l1 * m[2], m[4] - l2 * m[2]
        i2 = 1.0 / d2
        l3 = f2 * i2
        d3 = m[5] - l2 * m[3] - l3 * f2
        g1 = m[1] - l1 * m[0]
        c2 = (m[2] - l2 * m[0] - l3 * g1) / d3
        c1 = g1 * i2 - l3 * c2
        c0 = m[0] * i1 - l1 * c1 - l2 * c2
        coefficient.append([jnp.concatenate([SCALE * c, SCALE * c], axis=1) for c in (c0, c1, c2)])

    def finish(chunk, carry):
        for i in range(step):
            p = chunk * step + i
            for r in range(0, height, 8):
                s = pl.ds(r, 8)
                potential = []
                for job in range(2):
                    value = coefficient[job][0] * field[0, job, p + 1, s]
                    for gen in range(1, ITERS):
                        value = value + coefficient[job][gen] * field[gen, job, p + 1, s]
                    potential.append(value)
                near, far, third = o[0, p, s], o[1, p, s], o[2, p, s]
                u_out[p, s] = -(potential[1] * far)
                far_out[p, s] = -(potential[0] * near + potential[1] * third)
                near_out[p, s] = -(potential[0] * far)
        remote(far_out.at[part(chunk)], out.at[0, part(chunk), mine], out_s.at[chunk], out_r.at[chunk], across).start()
        remote(u_out.at[part(chunk)], u_in.at[part(chunk)], u_s.at[chunk], u_r.at[chunk], aside).start()
        return carry

    lax.fori_loop(0, CHUNKS, finish, 0)

    def near_copy(chunk):
        return pltpu.make_async_copy(near_out.at[part(chunk)], out.at[0, part(chunk), mine], near_s.at[chunk])

    def finish_near(chunk, carry):
        arrived(u_in.at[part(chunk)], u_r.at[chunk])
        for i in range(step):
            p = chunk * step + i
            near_out[p] = near_out[p] + u_in[p]
        near_copy(chunk).start()
        return carry

    lax.fori_loop(0, CHUNKS, finish_near, 0)

    for chunk in range(CHUNKS):
        arrived(out.at[0, part(chunk), theirs], out_r.at[chunk])
        near_copy(chunk).wait()
        sent(far_out.at[part(chunk)], out_s.at[chunk])
        sent(u_out.at[part(chunk)], u_s.at[chunk])
        sent(orb.at[0, part(chunk), theirs], far_s.at[chunk])
        sent(orb.at[0, part(chunk), mine], third_s.at[chunk])
    for copy in eps_planes:
        copy.wait_send()
    for gen in range(ITERS):
        for job in range(2):
            for copy in halo_planes(gen, job) + halo_rows(gen, job):
                copy.wait_send()
    for d in range(cz - 1):
        sent(red, z_s.at[d])
    for at in range(11):
        sent(yred, y_s.at[at])


def per_device(cx, cz, orbitals, dielectric):
    _, deep, width, lanes = orbitals.shape
    planes, height = deep, width // 2
    full = (planes, height, lanes)
    vmem, dma = pltpu.VMEM, pltpu.SemaphoreType.DMA
    scratch = [
        vmem((3, *full), F32),
        vmem((planes + 2, height, lanes), F32),
        vmem((planes, 8, lanes), F32),
        vmem((planes + 1, height, lanes), F32),
        vmem(full, F32),
        vmem(full, F32),
        vmem(full, F32),
        vmem(full, F32),
        vmem((ITERS, 2, planes + 2, height, lanes), F32),
        vmem((ITERS, 2, planes, 1, lanes), F32),
        vmem((ITERS, 2, planes, 1, lanes), F32),
        vmem((2, planes, 1, lanes), F32),
        vmem((16, lanes // 2), F32),
        vmem((cz - 1, 16, lanes // 2), F32),
        vmem((16, lanes // 2), F32),
        vmem((11, 16, lanes // 2), F32),
        vmem(full, F32),
        vmem(full, F32),
        vmem(full, F32),
        vmem(full, F32),
        dma,
        *[dma((CHUNKS,))] * 4,
        dma((2,)),
        *[dma((ITERS + 1, 2, 2))] * 2,
        *[dma((ITERS, 2))] * 2,
        *[dma((cz - 1,))] * 2,
        *[dma((11,))] * 2,
        *[dma((CHUNKS,))] * 5,
    ]
    return pl.pallas_call(
        functools.partial(kernel, cx, cz),
        out_shape=jax.ShapeDtypeStruct(orbitals.shape, F32),
        in_specs=[pl.BlockSpec(memory_space=pl.ANY)] * 2,
        out_specs=pl.BlockSpec(memory_space=pl.ANY),
        scratch_shapes=scratch,
        compiler_params=pltpu.CompilerParams(
            collective_id=0, has_side_effects=True, vmem_limit_bytes=60 * 1024 * 1024
        ),
    )(orbitals, dielectric)


def solution(mesh):
    return jax.shard_map(
        functools.partial(per_device, mesh.shape["blk"] // 2, mesh.shape["dom"] // 4),
        mesh=mesh,
        in_specs=(P("blk", "dom", None, None), P("dom", None, None)),
        out_specs=P("blk", "dom", None, None),
        check_vma=False,
    )
```

```python
import functools
import math

import jax
import jax.numpy as jnp
from jax import lax
from jax.experimental import pallas as pl
from jax.experimental.pallas import tpu as pltpu
from jax.sharding import PartitionSpec as P

FOUR_PI = 4.0 * math.pi
ITERS = 3
SCALE = 1.0 / 16.0
CHUNKS = 4
AHEAD = 2
SEQUENCE = (0, 3, 1, 2)
STRIP = 16
F32 = jnp.float32


def kernel(cx, cz, orb, eps, out, *scratch):
    (o, e, eblock, wx, wyp, wym, wzp, wzm, field, pack, rows, erows, red, zin, yred, yin, far_out, near_out, u_out, u_in,
     own_s, far_s, far_r, third_s, third_r, eps_s, plane_s, plane_r, row_s, row_r, z_s, z_r, y_s, y_r, near_s, out_s,
     out_r, u_s, u_r) = scratch
    planes, height, lanes = o.shape[1:]
    step = planes // CHUNKS
    blk, dom = lax.axis_index("blk"), lax.axis_index("dom")
    x, yh = blk // 2, blk % 2
    z, yl, core = dom // 4, (dom // 2) % 2, dom % 2
    dx = 1 - 2 * yh

    def flip(value, by):
        return value + by - 2 * by * value if by else value

    def device(x_, yh_, z_, yl_, core_):
        x_, z_ = lax.rem(x_ + cx, cx), lax.rem(z_ + cz, cz)
        return {"blk": x_ * 2 + yh_, "dom": z_ * 4 + yl_ * 2 + core_}

    def remote(src, dst, send, recv, to):
        return pltpu.make_async_remote_copy(src_ref=src, dst_ref=dst, send_sem=send, recv_sem=recv, device_id=to)

    def arrived(dst, recv):
        pltpu.make_async_copy(dst, dst, recv).wait()

    def sent(src, send):
        pltpu.make_async_copy(src, src, send).wait()

    barrier = pltpu.get_barrier_semaphore()
    partners = []
    for k in range(4):
        for cc in range(2):
            if k or cc:
                partners.append(device(x, flip(yh, k // 2), z, flip(yl, k % 2), flip(core, cc)))
    partners += [device(x + 1, yh, z, yl, core), device(x - 1, yh, z, yl, core)]
    partners += [device(x, yh, z + d, yl, core) for d in range(1, cz)]
    below, above = lax.rem(dom + 4 * cz - 1, 4 * cz), lax.rem(dom + 1, 4 * cz)
    to_plane = {"blk": blk, "dom": below}, {"blk": blk, "dom": above}
    partners += to_plane
    for k in range(2):
        for cc in range(2):
            partners.append(device(x + dx, 1 - yh, z, flip(yl, k), flip(core, cc)))
    for partner in partners:
        pl.semaphore_signal(barrier, inc=1, device_id=partner)
    pl.semaphore_wait(barrier, len(partners))

    across, aside, back = device(x, 1 - yh, z, yl, core), device(x + dx, yh, z, yl, core), device(x - dx, yh, z, yl, core)
    mine, theirs = pl.ds(height * yh, height), pl.ds(height * (1 - yh), height)

    def part(chunk):
        return pl.ds(chunk * step, step)

    def send(chunk):
        remote(orb.at[0, part(chunk), theirs], o.at[1, part(chunk)], far_s.at[chunk], far_r.at[chunk], across).start()
        remote(orb.at[0, part(chunk), mine], o.at[2, part(chunk)], third_s.at[chunk], third_r.at[chunk], back).start()

    for chunk in SEQUENCE[:AHEAD]:
        send(chunk)
    local = [
        pltpu.make_async_copy(eps.at[:, mine], e.at[pl.ds(1, planes)], eps_s.at[0]),
        pltpu.make_async_copy(eps.at[:, pl.ds(height - 8 * yh, 8)], eblock, eps_s.at[1]),
        pltpu.make_async_copy(orb.at[0, :, mine], o.at[0], own_s),
    ]
    for copy in local:
        copy.start()

    to_row = across, device(x + dx, 1 - yh, z, yl, core)
    first_plane, last_plane = dom == 0, dom == 4 * cz - 1
    has_after = jnp.where(yh == 0, 1.0, 0.0)
    has_before = 1.0 - has_after

    def plane_copies(gen, job, lower, upper, lower_to, upper_to):
        return [remote(lower, upper_to, plane_s.at[gen, job, 0], plane_r.at[gen, job, 0], to_plane[0]),
                remote(upper, lower_to, plane_s.at[gen, job, 1], plane_r.at[gen, job, 1], to_plane[1])]

    def halo_planes(gen, job):
        f = field.at[gen, job]
        return plane_copies(gen, job, f.at[1], f.at[planes], f.at[0], f.at[planes + 1])

    def halo_rows(gen, job):
        return [remote(pack.at[gen, job], rows.at[gen, job], row_s.at[gen, job], row_r.at[gen, job], to_row[job])]

    def start(copies):
        for copy in copies:
            copy.start()

    def finish_planes(gen, job):
        for side, edge, at in ((0, last_plane, planes + 1), (1, first_plane, 0)):
            arrived(field.at[gen, job, at], plane_r.at[gen, job, side])

            @pl.when(edge)
            def _():
                field[gen, job, at] = jnp.zeros((height, lanes), F32)

    local[0].wait()
    eps_planes = plane_copies(ITERS, 0, e.at[1], e.at[planes], e.at[0], e.at[planes + 1])
    start(eps_planes)
    local[1].wait()
    erows[0] = eblock[:, 7:8] * has_before
    erows[1] = eblock[:, 0:1] * has_after
    for side, edge, at in ((0, last_plane, planes + 1), (1, first_plane, 0)):
        arrived(e.at[at], plane_r.at[ITERS, 0, side])

        @pl.when(edge)
        def _():
            e[at] = jnp.zeros((height, lanes), F32)

    row_at = lax.broadcasted_iota(jnp.int32, (STRIP, lanes), 0)
    lane_at = lax.broadcasted_iota(jnp.int32, (STRIP, lanes), 1)

    def four(value, before, after):
        below = jnp.where(row_at == STRIP - 1, after, pltpu.roll(value, STRIP - 1, 0))
        above = jnp.where(row_at == 0, before, pltpu.roll(value, 1, 0))
        right = jnp.where(lane_at == lanes - 1, 0.0, pltpu.roll(value, lanes - 1, 1))
        left = jnp.where(lane_at == 0, 0.0, pltpu.roll(value, 1, 1))
        return below, above, right, left

    def weigh(p, carry):
        for r in range(0, height, STRIP):
            s = pl.ds(r, STRIP)
            value = e[p + 1, s]
            before = e[p + 1, r - 1 : r] if r else erows[0, p]
            after = e[p + 1, r + STRIP : r + STRIP + 1] if r + STRIP < height else erows[1, p]
            below, above, right, left = four(value, before, after)
            wyp[p, s] = (value + below) * (0.5 * SCALE)
            wym[p, s] = (value + above) * (0.5 * SCALE)
            wzp[p, s] = (value + right) * (0.5 * SCALE)
            wzm[p, s] = (value + left) * (0.5 * SCALE)
            wx[p, s] = (value + e[p, s]) * (0.5 * SCALE)
        return carry

    lax.fori_loop(0, planes, weigh, 0)
    wx[planes] = (e[planes] + e[planes + 1]) * (0.5 * SCALE)
    local[2].wait()

    def density(job, chunk):
        for i in range(step):
            p = chunk * step + i
            value = FOUR_PI * o[1, p] * o[2 * job, p]
            field[0, job, p + 1] = value
            pack[0, job, p] = value[height - 1 : height] * has_after + value[0:1] * has_before

    def second_density(n, chunk):
        arrived(o.at[2, part(chunk)], third_r.at[chunk])
        density(1, chunk)
        if n < 2:
            start(halo_planes(0, 1)[n : n + 1])

    for n, chunk in enumerate(SEQUENCE):
        arrived(o.at[1, part(chunk)], far_r.at[chunk])
        if n + AHEAD < CHUNKS:
            send(SEQUENCE[n + AHEAD])
        density(0, chunk)
        if n < 2:
            start(halo_planes(0, 0)[n : n + 1])
        if n < CHUNKS - 1:
            second_density(n, chunk)

    start(halo_rows(0, 0))

    def folded(value):
        total = value[0:8]
        for r in range(8, STRIP, 8):
            total = total + value[r : r + 8]
        return total[:, : lanes // 2] + total[:, lanes // 2 :]

    def apply(gen, job, strips, p, sums):
        first_sum, second_sum = sums
        for r in strips:
            s = pl.ds(r, STRIP)
            value = field[gen, job, p + 1, s]
            before = field[gen, job, p + 1, r - 1 : r] if r else rows[gen, job, p] * has_before
            last = r + STRIP == height
            after = rows[gen, job, p] * has_after if last else field[gen, job, p + 1, r + STRIP : r + STRIP + 1]
            below, above, right, left = four(value, before, after)
            result = wx[p + 1, s] * (value - field[gen, job, p + 2, s])
            result += wx[p, s] * (value - field[gen, job, p, s])
            result += wyp[p, s] * (value - below)
            result += wym[p, s] * (value - above)
            result += wzp[p, s] * (value - right)
            result += wzm[p, s] * (value - left)
            if gen < ITERS - 1:
                field[gen + 1, job, p + 1, s] = result
                if r == 0:
                    pack[gen + 1, job, p] = result[0:1] * has_before
                if last:
                    pack[gen + 1, job, p] += result[STRIP - 1 : STRIP] * has_after
            first_sum += folded(value * value)
            second_sum += folded(value * result)
        return first_sum, second_sum

    half_lanes = lanes // 2
    tile_row = lax.broadcasted_iota(jnp.int32, (16, half_lanes), 0)
    strips = list(range(0, height, STRIP))

    tile = jnp.zeros((16, half_lanes), F32)

    def power(gen, job, tile):
        sums = (jnp.zeros((8, half_lanes), F32),) * 2
        sums = lax.fori_loop(1, planes - 1, functools.partial(apply, gen, job, strips[1:-1]), sums)
        if gen == job == 0:
            second_density(CHUNKS - 1, SEQUENCE[-1])
            start(halo_rows(0, 1))
        arrived(rows.at[gen, job], row_r.at[gen, job])
        sums = lax.fori_loop(1, planes - 1, functools.partial(apply, gen, job, (strips[0], strips[-1])), sums)
        finish_planes(gen, job)
        sums = lax.fori_loop(0, 2, lambda i, c: apply(gen, job, strips, i * (planes - 1), c), sums)
        if gen < ITERS - 1:
            start(halo_planes(gen + 1, job))
            start(halo_rows(gen + 1, job))
        for q in range(2):
            moment = jnp.sum(sums[q], axis=0, keepdims=True)
            tile = jnp.where(tile_row == 8 * job + 2 * gen + q, moment, tile)
        return tile

    for gen in range(ITERS):
        for job in range(2):
            tile = power(gen, job, tile)

    red[...] = tile
    for d in sorted(range(1, cz), key=lambda d: -min(d, cz - d)):
        remote(red, zin.at[d - 1], z_s.at[d - 1], z_r.at[d - 1], device(x, yh, z + d, yl, core)).start()
    for d in range(1, cz):
        arrived(zin.at[d - 1], z_r.at[d - 1])
        tile = tile + zin[d - 1]
    yred[...] = tile
    relations = [(x_, h, k, cc) for x_, h in ((0, 0), (0, 1), (1, 1)) for k in range(2) for cc in range(2)][1:]
    for at, (x_, h, k, cc) in reversed(list(enumerate(relations))):
        remote(yred, yin.at[at], y_s.at[at], y_r.at[at],
               device(x + dx * x_, flip(yh, h), z, flip(yl, k), flip(core, cc))).start()
    for at, (x_, h, k, cc) in enumerate(relations):
        arrived(yin.at[at], y_r.at[at])
        other = yin[at]
        if h:
            other = jnp.where((tile_row // 8) == x_, other, 0.0)
        tile = tile + other

    total = jnp.broadcast_to(jnp.sum(tile, axis=1, keepdims=True), (16, half_lanes))
    coefficient = []
    for job in range(2):
        m = [jnp.broadcast_to(total[8 * job + k : 8 * job + k + 1], (8, half_lanes)) for k in range(6)]
        i1 = 1.0 / m[1]
        l1, l2 = m[2] * i1, m[3] * i1
        d2, f2 = m[3] - l1 * m[2], m[4] - l2 * m[2]
        i2 = 1.0 / d2
        l3 = f2 * i2
        d3 = m[5] - l2 * m[3] - l3 * f2
        g1 = m[1] - l1 * m[0]
        c2 = (m[2] - l2 * m[0] - l3 * g1) / d3
        c1 = g1 * i2 - l3 * c2
        c0 = m[0] * i1 - l1 * c1 - l2 * c2
        coefficient.append([jnp.concatenate([SCALE * c, SCALE * c], axis=1) for c in (c0, c1, c2)])

    def finish(chunk, carry):
        for i in range(step):
            p = chunk * step + i
            for r in range(0, height, 8):
                s = pl.ds(r, 8)
                potential = []
                for job in range(2):
                    value = coefficient[job][0] * field[0, job, p + 1, s]
                    for gen in range(1, ITERS):
                        value = value + coefficient[job][gen] * field[gen, job, p + 1, s]
                    potential.append(value)
                near, far, third = o[0, p, s], o[1, p, s], o[2, p, s]
                u_out[p, s] = -(potential[1] * far)
                far_out[p, s] = -(potential[0] * near + potential[1] * third)
                near_out[p, s] = -(potential[0] * far)
        remote(far_out.at[part(chunk)], out.at[0, part(chunk), mine], out_s.at[chunk], out_r.at[chunk], across).start()
        remote(u_out.at[part(chunk)], u_in.at[part(chunk)], u_s.at[chunk], u_r.at[chunk], aside).start()
        return carry

    lax.fori_loop(0, CHUNKS, finish, 0)

    def near_copy(chunk):
        return pltpu.make_async_copy(near_out.at[part(chunk)], out.at[0, part(chunk), mine], near_s.at[chunk])

    def finish_near(chunk, carry):
        arrived(u_in.at[part(chunk)], u_r.at[chunk])
        for i in range(step):
            p = chunk * step + i
            near_out[p] = near_out[p] + u_in[p]
        near_copy(chunk).start()
        return carry

    lax.fori_loop(0, CHUNKS, finish_near, 0)

    for chunk in range(CHUNKS):
        arrived(out.at[0, part(chunk), theirs], out_r.at[chunk])
        near_copy(chunk).wait()
        sent(far_out.at[part(chunk)], out_s.at[chunk])
        sent(u_out.at[part(chunk)], u_s.at[chunk])
        sent(orb.at[0, part(chunk), theirs], far_s.at[chunk])
        sent(orb.at[0, part(chunk), mine], third_s.at[chunk])
    for copy in eps_planes:
        copy.wait_send()
    for gen in range(ITERS):
        for job in range(2):
            for copy in halo_planes(gen, job) + halo_rows(gen, job):
                copy.wait_send()
    for d in range(cz - 1):
        sent(red, z_s.at[d])
    for at in range(11):
        sent(yred, y_s.at[at])


def per_device(cx, cz, orbitals, dielectric):
    _, deep, width, lanes = orbitals.shape
    planes, height = deep, width // 2
    full = (planes, height, lanes)
    vmem, dma = pltpu.VMEM, pltpu.SemaphoreType.DMA
    scratch = [
        vmem((3, *full), F32),
        vmem((planes + 2, height, lanes), F32),
        vmem((planes, 8, lanes), F32),
        vmem((planes + 1, height, lanes), F32),
        vmem(full, F32),
        vmem(full, F32),
        vmem(full, F32),
        vmem(full, F32),
        vmem((ITERS, 2, planes + 2, height, lanes), F32),
        vmem((ITERS, 2, planes, 1, lanes), F32),
        vmem((ITERS, 2, planes, 1, lanes), F32),
        vmem((2, planes, 1, lanes), F32),
        vmem((16, lanes // 2), F32),
        vmem((cz - 1, 16, lanes // 2), F32),
        vmem((16, lanes // 2), F32),
        vmem((11, 16, lanes // 2), F32),
        vmem(full, F32),
        vmem(full, F32),
        vmem(full, F32),
        vmem(full, F32),
        dma,
        *[dma((CHUNKS,))] * 4,
        dma((2,)),
        *[dma((ITERS + 1, 2, 2))] * 2,
        *[dma((ITERS, 2))] * 2,
        *[dma((cz - 1,))] * 2,
        *[dma((11,))] * 2,
        *[dma((CHUNKS,))] * 5,
    ]
    return pl.pallas_call(
        functools.partial(kernel, cx, cz),
        out_shape=jax.ShapeDtypeStruct(orbitals.shape, F32),
        in_specs=[pl.BlockSpec(memory_space=pl.ANY)] * 2,
        out_specs=pl.BlockSpec(memory_space=pl.ANY),
        scratch_shapes=scratch,
        compiler_params=pltpu.CompilerParams(
            collective_id=0, has_side_effects=True, vmem_limit_bytes=60 * 1024 * 1024
        ),
    )(orbitals, dielectric)


def solution(mesh):
    return jax.shard_map(
        functools.partial(per_device, mesh.shape["blk"] // 2, mesh.shape["dom"] // 4),
        mesh=mesh,
        in_specs=(P("blk", "dom", None, None), P("dom", None, None)),
        out_specs=P("blk", "dom", None, None),
        check_vma=False,
    )
```
